32 devices in a mesh: grp: 2 (over x), blk: 8 (over z, y), sum: 2 (over core).
Axes of the slice: x: 2, y: 2, z: 4, core: 2. Of those that a mesh axis runs over, the one named last changes fastest.
Arguments:
- points: bfloat16 [32768, 512], P(('grp', 'blk')), parts along dimension 0, may hold values from -6 to 6
- centers: bfloat16 [2048, 512], P(('blk', 'sum')), may hold values from -6 to 6
- coefficients: bfloat16 [2048, 256], P(('blk', 'sum')), may hold values from -60 to 60
- targets: float32 [32768, 256], P(('grp', 'blk'), 'sum'), parts along dimension 0, may hold values from -6 to 6
Outputs:
- residual: float32 [32768, 256], P(('grp', 'blk'), 'sum'), parts along dimension 0
The draws below stay inside these ranges and needn't reach their ends.
There are 2 independent parts, one for each index of `grp`. The reference program is written for one: setup_inputs(seed, part) draws one part's arguments, and reference() takes and returns one part's arrays. A program takes and returns all parts, laid end to end along the dimension named above; an argument that names none is the same for every part. Nothing has to cross between parts.
All inputs are finite; a program needn't handle non-finite values.
Results may differ from the reference program's by a relative error of at most 0.0029.
Values may be sent and summed in bfloat16 or wider, within the bound.
A program may use at most 64 MiB of HBM per device.

```python
import math
import jax
import jax.numpy as jnp
from jax import lax

F = 512
O = 256
NPTS = 16384
CENTERS = 2048


def shard_levels(rng, dims, shards, least, high):
    def one(axis_at, shards_of):
        draws = jax.random.uniform(jax.random.fold_in(jax.random.fold_in(rng, 6), axis_at), (shards_of,), jnp.float32, least / len(shards), high / len(shards))
        return jnp.repeat(jnp.exp(draws), dims[axis_at] // shards_of).reshape((-1,) + (1,) * (len(dims) - axis_at - 1))

    level = one(*shards[0])
    for cut in shards[1:]:
        level = level * one(*cut)
    return level


def gaussian(key, extent, width, bound, shards=(), kind=jnp.bfloat16):
    level = shard_levels(key, extent, shards, -0.22, 0.18) if shards else 1.0
    values = jax.random.normal(key, extent, jnp.float32) * width * level
    return jnp.minimum(jnp.maximum(values, -bound), bound).astype(kind)


def setup_inputs(seed: int = 0, part: int = 0) -> dict:
    keys = jax.random.split(jax.random.key(seed), 5)
    part_keys = jax.random.split(jax.random.fold_in(keys[4], part), 5)
    points = gaussian(part_keys[0], (NPTS, F), 1.0, 6.0, ((0, 8),))
    centers = gaussian(keys[1], (CENTERS, F), 1.0, 6.0, ((0, 16),))
    coefficients = gaussian(keys[2], (CENTERS, O), 10.0, 60.0, ((0, 16),))
    targets = gaussian(part_keys[3], (NPTS, O), 1.0, 6.0, ((0, 8), (1, 2)), jnp.float32)
    return dict(points=points, centers=centers, coefficients=coefficients, targets=targets)


def reference(points, centers, coefficients, targets):
    sharpness = 0.15 / math.sqrt(F)
    point_sq = lax.optimization_barrier(jnp.sum(jnp.square(points.astype(jnp.float32)), axis=1))
    block_rows = math.gcd(CENTERS, 256)
    block_count = CENTERS // block_rows
    center_blocks = centers.reshape(block_count, block_rows, F)
    coef_blocks = coefficients.reshape(block_count, block_rows, O)

    def step(running, pieces):
        center_block, coef_block = pieces
        products = jnp.dot(points, center_block.T, preferred_element_type=jnp.float32)
        center_sq = lax.optimization_barrier(jnp.sum(jnp.square(center_block.astype(jnp.float32)), axis=1))
        kernel = jnp.exp(-sharpness * (point_sq[:, None] + center_sq[None, :] - 2.0 * products)).astype(jnp.bfloat16)
        return (running + jnp.dot(kernel, coef_block, preferred_element_type=jnp.float32), None)
    start_sum = jnp.zeros((NPTS, O), jnp.float32)
    predicted, _ = lax.scan(step, start_sum, (center_blocks, coef_blocks))
    return targets - predicted
```

```python
import functools
import math

import jax
import jax.numpy as jnp
from jax import lax
from jax.experimental import pallas as pl
from jax.experimental.pallas import tpu as pltpu
from jax.sharding import PartitionSpec as P

MESH = pl.DeviceIdType.MESH
TILE = 512
CHUNKS = 4


def ring_position(index, n):
    return jnp.where(lax.rem(index, 2) == 0, index // 2, n - 1 - index // 2) if n <= 8 else index


def ring_index(position, n):
    return jnp.where(position < n // 2, 2 * position, 2 * (n - 1 - position) + 1) if n <= 8 else position


def body(n, cross, points_hbm, centers_hbm, coef_hbm, out_ref,
         points, held, point_term, total, landed,
         local_sem, ring_send, ring_recv, x_send, x_recv, swap_send, swap_recv):
    rows, features = points.shape
    block = held.shape[1]
    columns = total.shape[2]
    half = n // 2
    me = ring_position(lax.axis_index("blk"), n)
    right = ring_index(lax.rem(me + 1, n), n)
    left = ring_index(lax.rem(me + n - 1, n), n)
    mine = lax.axis_index("sum")
    other = 1 - mine
    group = lax.axis_index("grp")
    side = lax.rem(group, 2)
    sharpness = 0.15 / math.sqrt(features)
    scale = -sharpness * math.log2(math.e)

    copies = [
        pltpu.make_async_copy(centers_hbm, held.at[0, :, pl.ds(0, features)], local_sem.at[0]),
        pltpu.make_async_copy(coef_hbm, held.at[0, :, pl.ds(features, 2 * columns)], local_sem.at[1]),
        pltpu.make_async_copy(points_hbm, points, local_sem.at[2]),
    ]
    for copy in copies:
        copy.start()

    barrier = pltpu.get_barrier_semaphore()
    greet = [{"blk": left}, {"blk": right}, {"sum": other}]
    partner = {"grp": group + 1 - 2 * side}
    if cross:
        greet.append(partner)
    for device in greet:
        pl.semaphore_signal(barrier, inc=1, device_id=device, device_id_type=MESH)
    pl.semaphore_wait(barrier, len(greet))

    only = (3 * block // 8) // 16 * 16
    both = block - 2 * only
    if cross:
        parts = (pl.ds(pl.multiple_of(side * (only + both), 16), only), pl.ds(only, both))
    else:
        parts = (pl.ds(0, block // 2), pl.ds(block // 2, block // 2))

    def slot(way, d):
        if d == 0:
            return 0
        return n - 1 if d == half else 2 * d - 1 + way

    ring = {}
    for d in range(1, half + 1):
        for way in (0, 1):
            for part in (0, 1):
                if d == half and part != way:
                    continue
                ring[way, d, part] = pltpu.make_async_remote_copy(
                    src_ref=held.at[slot(way, d - 1), parts[part]],
                    dst_ref=held.at[slot(way, d), parts[part]],
                    send_sem=ring_send.at[way, d - 1, part],
                    recv_sem=ring_recv.at[way, d - 1, part],
                    device_id={"blk": (right, left)[way]},
                    device_id_type=MESH,
                )
    over = {}
    if cross:
        for s in range(1, n):
            over[s] = pltpu.make_async_remote_copy(
                src_ref=held.at[s, parts[0]], dst_ref=held.at[s, parts[0]],
                send_sem=x_send.at[s], recv_sem=x_recv.at[s],
                device_id=partner, device_id_type=MESH,
            )

    def row_sums(a, b):
        return lax.dot_general(a, b, (((1,), (1,)), ((), ())), preferred_element_type=jnp.float32)

    def split_square(v):
        square = jnp.square(v.astype(jnp.float32))
        high = square.astype(jnp.bfloat16)
        return high, (square - high.astype(jnp.float32)).astype(jnp.bfloat16)

    def prepare(first, count):
        size = count * block
        c = held[first:first + count, :, 0:features].reshape(size, features)
        w = held[first:first + count, :, features:features + 2 * columns].reshape(size, 2 * columns)
        high, low = split_square(c)
        ones = jnp.ones((16, features), jnp.bfloat16)
        term = scale * (row_sums(ones, high) + row_sums(ones, low))[0:1, :]
        return c, w, term

    def tile_sum(c, w, term, at, tile):
        products = row_sums(points[pl.ds(at, tile), :], c)
        a = point_term[pl.ds(at, tile), :]
        pieces = []
        for lane in range(0, c.shape[0], 128):
            exponent = (a + term[:, lane:lane + 128]) - (2.0 * scale) * products[:, lane:lane + 128]
            pieces.append(jnp.exp2(exponent).astype(jnp.bfloat16))
        kernel = pieces[0] if len(pieces) == 1 else jnp.concatenate(pieces, axis=1)
        return jnp.dot(kernel, w, preferred_element_type=jnp.float32)

    def group_sum(first, count, fresh):
        c, w, term = prepare(first, count)

        @pl.loop(0, rows // TILE)
        def _(i):
            at = pl.multiple_of(i * TILE, TILE)
            got = tile_sum(c, w, term, at, TILE)
            for h in (0, 1):
                piece = got[:, h * columns:(h + 1) * columns]
                if fresh:
                    total[h, pl.ds(at, TILE), :] = piece
                else:
                    total[h, pl.ds(at, TILE), :] += piece

    copies[0].wait()
    copies[1].wait()
    for part in (0, 1):
        for way in (0, 1):
            if (way, 1, part) in ring:
                ring[way, 1, part].start()

    copies[2].wait()

    @pl.loop(0, rows // TILE)
    def _(i):
        at = pl.multiple_of(i * TILE, TILE)
        high, low = split_square(points[pl.ds(at, TILE), :])
        ones = jnp.ones((128, features), jnp.bfloat16)
        point_term[pl.ds(at, TILE), :] = scale * (row_sums(high, ones) + row_sums(low, ones))

    group_sum(0, 1, True)
    for d in range(1, half + 1):
        for part in (0, 1):
            for way in (0, 1):
                if (way, d, part) not in ring:
                    continue
                ring[way, d, part].wait_recv()
                if (way, d + 1, part) in ring:
                    ring[way, d + 1, part].start()
                if cross and part == 0:
                    over[slot(way, d)].start()
        if d > 1:
            if cross:
                over[slot(0, d - 1)].wait_recv()
                over[slot(1, d - 1)].wait_recv()
            group_sum(slot(0, d - 1), 2, False)

    if cross:
        over[n - 1].wait_recv()
    c, w, term = prepare(n - 1, 1)
    size = rows // CHUNKS
    swaps = []
    for i in range(CHUNKS):
        got = tile_sum(c, w, term, i * size, size)
        for h in (0, 1):
            total[h, i * size:(i + 1) * size, :] += got[:, h * columns:(h + 1) * columns]
        swap = pltpu.make_async_remote_copy(
            src_ref=total.at[other, pl.ds(i * size, size)],
            dst_ref=landed.at[pl.ds(i * size, size)],
            send_sem=swap_send.at[i], recv_sem=swap_recv.at[i],
            device_id={"sum": other}, device_id_type=MESH,
        )
        swap.start()
        swaps.append(swap)
    for i in range(CHUNKS):
        swaps[i].wait_recv()
        at = pl.ds(i * size, size)
        out_ref[at, :] = total[mine, at, :] + landed[at, :]
    for copy in (*ring.values(), *over.values(), *swaps):
        copy.wait_send()


def per_device(n, cross, points, centers, coefficients, targets):
    rows, features = points.shape
    block = centers.shape[0]
    width = coefficients.shape[1]
    columns = targets.shape[1]
    half = n // 2
    predicted = pl.pallas_call(
        functools.partial(body, n, cross),
        out_shape=jax.ShapeDtypeStruct((rows, columns), jnp.float32),
        in_specs=[pl.BlockSpec(memory_space=pltpu.HBM)] * 3,
        out_specs=pl.BlockSpec(memory_space=pltpu.VMEM),
        scratch_shapes=[
            pltpu.VMEM((rows, features), jnp.bfloat16),
            pltpu.VMEM((n, block, features + width), jnp.bfloat16),
            pltpu.VMEM((rows, 128), jnp.float32),
            pltpu.VMEM((2, rows, columns), jnp.float32),
            pltpu.VMEM((rows, columns), jnp.float32),
            pltpu.SemaphoreType.DMA((3,)),
            pltpu.SemaphoreType.DMA((2, half, 2)),
            pltpu.SemaphoreType.DMA((2, half, 2)),
            pltpu.SemaphoreType.DMA((n,)),
            pltpu.SemaphoreType.DMA((n,)),
            pltpu.SemaphoreType.DMA((CHUNKS,)),
            pltpu.SemaphoreType.DMA((CHUNKS,)),
        ],
        compiler_params=pltpu.CompilerParams(
            collective_id=0, has_side_effects=True, vmem_limit_bytes=40 * 2**20
        ),
        cost_estimate=pl.CostEstimate(
            flops=2 * rows * n * block * (features + width),
            bytes_accessed=2 * rows * features + 4 * rows * columns,
            transcendentals=rows * n * block,
        ),
    )(points, centers, coefficients)
    return targets - predicted


def solution(mesh):
    return jax.shard_map(
        functools.partial(per_device, mesh.shape["blk"], mesh.shape["grp"] % 2 == 0),
        mesh=mesh,
        in_specs=(
            P(("grp", "blk"), None),
            P(("blk", "sum"), None),
            P(("blk", "sum"), None),
            P(("grp", "blk"), "sum"),
        ),
        out_specs=P(("grp", "blk"), "sum"),
        check_vma=False,
    )
```

```python
import functools
import math

import jax
import jax.numpy as jnp
from jax import lax
from jax.experimental import pallas as pl
from jax.experimental.pallas import tpu as pltpu
from jax.sharding import PartitionSpec as P

MESH = pl.DeviceIdType.MESH
TILE = 512
CHUNKS = 4
PIECES = ((16, 32), (32,))
FIRST = 2


def ring_position(index, n):
    return jnp.where(lax.rem(index, 2) == 0, index // 2, n - 1 - index // 2) if n <= 8 else index


def ring_index(position, n):
    return jnp.where(position < n // 2, 2 * position, 2 * (n - 1 - position) + 1) if n <= 8 else position


def body(n, cross, points_hbm, centers_hbm, coef_hbm, out_ref,
         points, held, point_term, total, landed,
         local_sem, ring_send, ring_recv, x_send, x_recv, swap_send, swap_recv):
    rows, features = points.shape
    block = held.shape[1]
    columns = total.shape[2]
    half = n // 2
    me = ring_position(lax.axis_index("blk"), n)
    right = ring_index(lax.rem(me + 1, n), n)
    left = ring_index(lax.rem(me + n - 1, n), n)
    mine = lax.axis_index("sum")
    other = 1 - mine
    group = lax.axis_index("grp")
    side = lax.rem(group, 2)
    sharpness = 0.15 / math.sqrt(features)
    scale = -sharpness * math.log2(math.e)

    copies = [
        pltpu.make_async_copy(centers_hbm, held.at[0, :, pl.ds(0, features)], local_sem.at[0]),
        pltpu.make_async_copy(coef_hbm, held.at[0, :, pl.ds(features, 2 * columns)], local_sem.at[1]),
        pltpu.make_async_copy(points_hbm, points, local_sem.at[2]),
    ]
    for copy in copies:
        copy.start()

    barrier = pltpu.get_barrier_semaphore()
    greet = [{"blk": left}, {"blk": right}, {"sum": other}]
    partner = {"grp": group + 1 - 2 * side}
    if cross:
        greet.append(partner)
    for device in greet:
        pl.semaphore_signal(barrier, inc=1, device_id=device, device_id_type=MESH)
    pl.semaphore_wait(barrier, len(greet))

    pieces = []
    start = 0
    only = sum(PIECES[0]) * block // 128
    base = side * (block - only) if cross else 0
    for size in (size * block // 128 for size in PIECES[0]):
        pieces.append((pl.ds(pl.multiple_of(base + start, 16), size), True))
        start += size
    start, end = only, block - only if cross else block
    sizes = [size * block // 128 for size in PIECES[1]]
    sizes[-1] = end - start - sum(sizes[:-1])
    for size in sizes:
        pieces.append((pl.ds(start, size), False))
        start += size
    count = len(pieces)

    def slot(way, d):
        if d == 0:
            return 0
        return n - 1 if d == half else 2 * d - 1 + way

    ring = {}
    for d in range(1, half + 1):
        for way in (0, 1):
            for part in range(count):
                if d == half and way != (part >= FIRST):
                    continue
                ring[way, d, part] = pltpu.make_async_remote_copy(
                    src_ref=held.at[slot(way, d - 1), pieces[part][0]],
                    dst_ref=held.at[slot(way, d), pieces[part][0]],
                    send_sem=ring_send.at[way, d - 1, part],
                    recv_sem=ring_recv.at[way, d - 1, part],
                    device_id={"blk": (right, left)[way]},
                    device_id_type=MESH,
                )
    over = {}
    if cross:
        for s in range(1, n):
            for part in range(len(PIECES[0])):
                over[s, part] = pltpu.make_async_remote_copy(
                    src_ref=held.at[s, pieces[part][0]], dst_ref=held.at[s, pieces[part][0]],
                    send_sem=x_send.at[s, part], recv_sem=x_recv.at[s, part],
                    device_id=partner, device_id_type=MESH,
                )

    def row_sums(a, b):
        return lax.dot_general(a, b, (((1,), (1,)), ((), ())), preferred_element_type=jnp.float32)

    def split_square(v):
        square = jnp.square(v.astype(jnp.float32))
        high = square.astype(jnp.bfloat16)
        return high, (square - high.astype(jnp.float32)).astype(jnp.bfloat16)

    def prepare(first, count):
        size = count * block
        c = held[first:first + count, :, 0:features].reshape(size, features)
        w = held[first:first + count, :, features:features + 2 * columns].reshape(size, 2 * columns)
        high, low = split_square(c)
        ones = jnp.ones((16, features), jnp.bfloat16)
        term = scale * (row_sums(ones, high) + row_sums(ones, low))[0:1, :]
        return c, w, term

    def tile_sum(c, w, term, at, tile):
        products = row_sums(points[pl.ds(at, tile), :], c)
        a = point_term[pl.ds(at, tile), :]
        parts = []
        for lane in range(0, c.shape[0], 128):
            exponent = (a + term[:, lane:lane + 128]) - (2.0 * scale) * products[:, lane:lane + 128]
            parts.append(jnp.exp2(exponent).astype(jnp.bfloat16))
        kernel = parts[0] if len(parts) == 1 else jnp.concatenate(parts, axis=1)
        return jnp.dot(kernel, w, preferred_element_type=jnp.float32)

    def group_sum(first, count, fresh):
        c, w, term = prepare(first, count)

        @pl.loop(0, rows // TILE)
        def _(i):
            at = pl.multiple_of(i * TILE, TILE)
            got = tile_sum(c, w, term, at, TILE)
            for h in (0, 1):
                piece = got[:, h * columns:(h + 1) * columns]
                if fresh:
                    total[h, pl.ds(at, TILE), :] = piece
                else:
                    total[h, pl.ds(at, TILE), :] += piece

    copies[0].wait()
    copies[1].wait()
    for part in range(count):
        for way in (0, 1):
            if (way, 1, part) in ring:
                ring[way, 1, part].start()

    copies[2].wait()

    @pl.loop(0, rows // TILE)
    def _(i):
        at = pl.multiple_of(i * TILE, TILE)
        high, low = split_square(points[pl.ds(at, TILE), :])
        ones = jnp.ones((128, features), jnp.bfloat16)
        point_term[pl.ds(at, TILE), :] = scale * (row_sums(high, ones) + row_sums(low, ones))

    group_sum(0, 1, True)
    for d in range(1, half + 1):
        for part in range(count):
            for way in (0, 1):
                if (way, d, part) not in ring:
                    continue
                ring[way, d, part].wait_recv()
                if (way, d + 1, part) in ring:
                    ring[way, d + 1, part].start()
                if cross and pieces[part][1]:
                    over[slot(way, d), part].start()
        if d > 1:
            if cross:
                for part in range(len(PIECES[0])):
                    over[slot(0, d - 1), part].wait_recv()
                    over[slot(1, d - 1), part].wait_recv()
            group_sum(slot(0, d - 1), 2, False)

    if cross:
        for part in range(len(PIECES[0])):
            over[n - 1, part].wait_recv()
    c, w, term = prepare(n - 1, 1)
    size = rows // CHUNKS
    swaps = []
    for i in range(CHUNKS):
        got = tile_sum(c, w, term, i * size, size)
        for h in (0, 1):
            total[h, i * size:(i + 1) * size, :] += got[:, h * columns:(h + 1) * columns]
        swap = pltpu.make_async_remote_copy(
            src_ref=total.at[other, pl.ds(i * size, size)],
            dst_ref=landed.at[pl.ds(i * size, size)],
            send_sem=swap_send.at[i], recv_sem=swap_recv.at[i],
            device_id={"sum": other}, device_id_type=MESH,
        )
        swap.start()
        swaps.append(swap)
    for i in range(CHUNKS):
        swaps[i].wait_recv()
        at = pl.ds(i * size, size)
        out_ref[at, :] = total[mine, at, :] + landed[at, :]
    for copy in (*ring.values(), *over.values(), *swaps):
        copy.wait_send()


def per_device(n, cross, points, centers, coefficients, targets):
    rows, features = points.shape
    block = centers.shape[0]
    width = coefficients.shape[1]
    columns = targets.shape[1]
    half = n // 2
    predicted = pl.pallas_call(
        functools.partial(body, n, cross),
        out_shape=jax.ShapeDtypeStruct((rows, columns), jnp.float32),
        in_specs=[pl.BlockSpec(memory_space=pl.ANY)] * 3,
        out_specs=pl.BlockSpec(memory_space=pltpu.VMEM),
        scratch_shapes=[
            pltpu.VMEM((rows, features), jnp.bfloat16),
            pltpu.VMEM((n, block, features + width), jnp.bfloat16),
            pltpu.VMEM((rows, 128), jnp.float32),
            pltpu.VMEM((2, rows, columns), jnp.float32),
            pltpu.VMEM((rows, columns), jnp.float32),
            pltpu.SemaphoreType.DMA((3,)),
            pltpu.SemaphoreType.DMA((2, half, len(PIECES[0]) + len(PIECES[1]))),
            pltpu.SemaphoreType.DMA((2, half, len(PIECES[0]) + len(PIECES[1]))),
            pltpu.SemaphoreType.DMA((n, len(PIECES[0]))),
            pltpu.SemaphoreType.DMA((n, len(PIECES[0]))),
            pltpu.SemaphoreType.DMA((CHUNKS,)),
            pltpu.SemaphoreType.DMA((CHUNKS,)),
        ],
        compiler_params=pltpu.CompilerParams(
            collective_id=0, has_side_effects=True, vmem_limit_bytes=60 * 2**20
        ),
        cost_estimate=pl.CostEstimate(
            flops=2 * rows * n * block * (features + width),
            bytes_accessed=2 * rows * features + 4 * rows * columns,
            transcendentals=rows * n * block,
        ),
    )(points, centers, coefficients)
    return targets - predicted


def solution(mesh):
    return jax.shard_map(
        functools.partial(per_device, mesh.shape["blk"], mesh.shape["grp"] % 2 == 0),
        mesh=mesh,
        in_specs=(
            P(("grp", "blk"), None),
            P(("blk", "sum"), None),
            P(("blk", "sum"), None),
            P(("grp", "blk"), "sum"),
        ),
        out_specs=P(("grp", "blk"), "sum"),
        check_vma=False,
    )
```

```python
import functools
import math

import jax
import jax.numpy as jnp
from jax import lax
from jax.experimental import pallas as pl
from jax.experimental.pallas import tpu as pltpu
from jax.sharding import PartitionSpec as P

MESH = pl.DeviceIdType.MESH
TILE = 512
CHUNKS = 4
PIECES = ((16, 32), (32,))
FIRST = 2


def ring_position(index, n):
    return jnp.where(lax.rem(index, 2) == 0, index // 2, n - 1 - index // 2) if n <= 8 else index


def ring_index(position, n):
    return jnp.where(position < n // 2, 2 * position, 2 * (n - 1 - position) + 1) if n <= 8 else position


def body(n, cross, points_hbm, centers_hbm, coef_hbm, out_ref,
         points, held, point_term, total, landed,
         local_sem, ring_send, ring_recv, x_send, x_recv, swap_send, swap_recv):
    rows, features = points.shape
    block = held.shape[1]
    columns = total.shape[2]
    half = n // 2
    me = ring_position(lax.axis_index("blk"), n)
    right = ring_index(lax.rem(me + 1, n), n)
    left = ring_index(lax.rem(me + n - 1, n), n)
    mine = lax.axis_index("sum")
    other = 1 - mine
    group = lax.axis_index("grp")
    side = lax.rem(group, 2)
    sharpness = 0.15 / math.sqrt(features)
    scale = -sharpness * math.log2(math.e)

    copies = [
        pltpu.make_async_copy(centers_hbm, held.at[0, :, pl.ds(0, features)], local_sem.at[0]),
        pltpu.make_async_copy(coef_hbm, held.at[0, :, pl.ds(features, 2 * columns)], local_sem.at[1]),
        pltpu.make_async_copy(points_hbm, points, local_sem.at[2]),
    ]
    for copy in copies:
        copy.start()

    barrier = pltpu.get_barrier_semaphore()
    greet = [{"blk": left}, {"blk": right}, {"sum": other}]
    partner = {"grp": group + 1 - 2 * side}
    if cross:
        greet.append(partner)
    for device in greet:
        pl.semaphore_signal(barrier, inc=1, device_id=device, device_id_type=MESH)
    pl.semaphore_wait(barrier, len(greet))

    pieces = []
    start = 0
    only = sum(PIECES[0]) * block // 128
    base = side * (block - only) if cross else 0
    for size in (size * block // 128 for size in PIECES[0]):
        pieces.append((pl.ds(pl.multiple_of(base + start, 16), size), True))
        start += size
    start, end = only, block - only if cross else block
    sizes = [size * block // 128 for size in PIECES[1]]
    sizes[-1] = end - start - sum(sizes[:-1])
    for size in sizes:
        pieces.append((pl.ds(start, size), False))
        start += size
    count = len(pieces)

    def slot(way, d):
        if d == 0:
            return 0
        return n - 1 if d == half else 2 * d - 1 + way

    ring = {}
    for d in range(1, half + 1):
        for way in (0, 1):
            for part in range(count):
                if d == half and way != (part >= FIRST):
                    continue
                ring[way, d, part] = pltpu.make_async_remote_copy(
                    src_ref=held.at[slot(way, d - 1), pieces[part][0]],
                    dst_ref=held.at[slot(way, d), pieces[part][0]],
                    send_sem=ring_send.at[way, d - 1, part],
                    recv_sem=ring_recv.at[way, d - 1, part],
                    device_id={"blk": (right, left)[way]},
                    device_id_type=MESH,
                )
    over = {}
    if cross:
        for s in range(1, n):
            for part in range(len(PIECES[0])):
                over[s, part] = pltpu.make_async_remote_copy(
                    src_ref=held.at[s, pieces[part][0]], dst_ref=held.at[s, pieces[part][0]],
                    send_sem=x_send.at[s, part], recv_sem=x_recv.at[s, part],
                    device_id=partner, device_id_type=MESH,
                )

    def row_sums(a, b):
        return lax.dot_general(a, b, (((1,), (1,)), ((), ())), preferred_element_type=jnp.float32)

    def split_square(v):
        square = jnp.square(v.astype(jnp.float32))
        high = square.astype(jnp.bfloat16)
        return high, (square - high.astype(jnp.float32)).astype(jnp.bfloat16)

    def prepare(first, count):
        size = count * block
        c = held[first:first + count, :, 0:features].reshape(size, features)
        w = held[first:first + count, :, features:features + 2 * columns].reshape(size, 2 * columns)
        high, low = split_square(c)
        ones = jnp.ones((16, features), jnp.bfloat16)
        term = scale * (row_sums(ones, high) + row_sums(ones, low))[0:1, :]
        return c, w, term

    def tile_sum(c, w, term, at, tile):
        products = row_sums(points[pl.ds(at, tile), :], c)
        a = point_term[pl.ds(at, tile), :]
        parts = []
        for lane in range(0, c.shape[0], 128):
            exponent = (a + term[:, lane:lane + 128]) - (2.0 * scale) * products[:, lane:lane + 128]
            parts.append(jnp.exp2(exponent).astype(jnp.bfloat16))
        kernel = parts[0] if len(parts) == 1 else jnp.concatenate(parts, axis=1)
        return jnp.dot(kernel, w, preferred_element_type=jnp.float32)

    def group_sum(first, count, fresh):
        c, w, term = prepare(first, count)

        @pl.loop(0, rows // TILE)
        def _(i):
            at = pl.multiple_of(i * TILE, TILE)
            got = tile_sum(c, w, term, at, TILE)
            for h in (0, 1):
                piece = got[:, h * columns:(h + 1) * columns]
                if fresh:
                    total[h, pl.ds(at, TILE), :] = piece
                else:
                    total[h, pl.ds(at, TILE), :] += piece

    copies[0].wait()
    copies[1].wait()
    for part in range(count):
        for way in (0, 1):
            if (way, 1, part) in ring:
                ring[way, 1, part].start()

    copies[2].wait()

    @pl.loop(0, rows // TILE)
    def _(i):
        at = pl.multiple_of(i * TILE, TILE)
        high, low = split_square(points[pl.ds(at, TILE), :])
        ones = jnp.ones((128, features), jnp.bfloat16)
        point_term[pl.ds(at, TILE), :] = scale * (row_sums(high, ones) + row_sums(low, ones))

    group_sum(0, 1, True)
    for d in range(1, half + 1):
        for part in range(count):
            for way in (0, 1):
                if (way, d, part) not in ring:
                    continue
                ring[way, d, part].wait_recv()
                if (way, d + 1, part) in ring:
                    ring[way, d + 1, part].start()
                if cross and pieces[part][1]:
                    over[slot(way, d), part].start()
        if d > 1:
            if cross:
                for part in range(len(PIECES[0])):
                    over[slot(0, d - 1), part].wait_recv()
                    over[slot(1, d - 1), part].wait_recv()
            group_sum(slot(0, d - 1), 2, False)

    if cross:
        for part in range(len(PIECES[0])):
            over[n - 1, part].wait_recv()
    c, w, term = prepare(n - 1, 1)
    size = rows // CHUNKS
    swaps = []
    for i in range(CHUNKS):
        got = tile_sum(c, w, term, i * size, size)
        for h in (0, 1):
            total[h, i * size:(i + 1) * size, :] += got[:, h * columns:(h + 1) * columns]
        swap = pltpu.make_async_remote_copy(
            src_ref=total.at[other, pl.ds(i * size, size)],
            dst_ref=landed.at[pl.ds(i * size, size)],
            send_sem=swap_send.at[i], recv_sem=swap_recv.at[i],
            device_id={"sum": other}, device_id_type=MESH,
        )
        swap.start()
        swaps.append(swap)
    for i in range(CHUNKS):
        swaps[i].wait_recv()
        at = pl.ds(i * size, size)
        out_ref[at, :] = total[mine, at, :] + landed[at, :]
    for copy in (*ring.values(), *over.values(), *swaps):
        copy.wait_send()


def per_device(n, cross, points, centers, coefficients, targets):
    rows, features = points.shape
    block = centers.shape[0]
    width = coefficients.shape[1]
    columns = targets.shape[1]
    half = n // 2
    predicted = pl.pallas_call(
        functools.partial(body, n, cross),
        out_shape=pltpu.VMEM((rows, columns), jnp.float32),
        in_specs=[pl.BlockSpec(memory_space=pl.ANY)] * 3,
        out_specs=pl.BlockSpec(memory_space=pltpu.VMEM),
        scratch_shapes=[
            pltpu.VMEM((rows, features), jnp.bfloat16),
            pltpu.VMEM((n, block, features + width), jnp.bfloat16),
            pltpu.VMEM((rows, 128), jnp.float32),
            pltpu.VMEM((2, rows, columns), jnp.float32),
            pltpu.VMEM((rows, columns), jnp.float32),
            pltpu.SemaphoreType.DMA((3,)),
            pltpu.SemaphoreType.DMA((2, half, len(PIECES[0]) + len(PIECES[1]))),
            pltpu.SemaphoreType.DMA((2, half, len(PIECES[0]) + len(PIECES[1]))),
            pltpu.SemaphoreType.DMA((n, len(PIECES[0]))),
            pltpu.SemaphoreType.DMA((n, len(PIECES[0]))),
            pltpu.SemaphoreType.DMA((CHUNKS,)),
            pltpu.SemaphoreType.DMA((CHUNKS,)),
        ],
        compiler_params=pltpu.CompilerParams(
            collective_id=0, has_side_effects=True, vmem_limit_bytes=58 * 2**20
        ),
        cost_estimate=pl.CostEstimate(
            flops=2 * rows * n * block * (features + width),
            bytes_accessed=2 * rows * features + 4 * rows * columns,
            transcendentals=rows * n * block,
        ),
    )(points, centers, coefficients)
    return targets - predicted


def solution(mesh):
    return jax.shard_map(
        functools.partial(per_device, mesh.shape["blk"], mesh.shape["grp"] % 2 == 0),
        mesh=mesh,
        in_specs=(
            P(("grp", "blk"), None),
            P(("blk", "sum"), None),
            P(("blk", "sum"), None),
            P(("grp", "blk"), "sum"),
        ),
        out_specs=P(("grp", "blk"), "sum"),
        check_vma=False,
    )
```

```python
import functools
import math

import jax
import jax.numpy as jnp
from jax import lax
from jax.experimental import pallas as pl
from jax.experimental.pallas import tpu as pltpu
from jax.sharding import PartitionSpec as P

MESH = pl.DeviceIdType.MESH
TILE = 1024
CHUNKS = 4
PIECES = ((16, 32), (32,))
FIRST = 2


def ring_position(index, n):
    return jnp.where(lax.rem(index, 2) == 0, index // 2, n - 1 - index // 2) if n <= 8 else index


def ring_index(position, n):
    return jnp.where(position < n // 2, 2 * position, 2 * (n - 1 - position) + 1) if n <= 8 else position


def body(n, cross, points_hbm, centers_hbm, coef_hbm, out_ref,
         points, held, point_term, total, landed,
         local_sem, ring_send, ring_recv, x_send, x_recv, swap_send, swap_recv):
    rows, features = points.shape
    block = held.shape[1]
    columns = total.shape[2]
    half = n // 2
    me = ring_position(lax.axis_index("blk"), n)
    right = ring_index(lax.rem(me + 1, n), n)
    left = ring_index(lax.rem(me + n - 1, n), n)
    mine = lax.axis_index("sum")
    other = 1 - mine
    group = lax.axis_index("grp")
    side = lax.rem(group, 2)
    sharpness = 0.15 / math.sqrt(features)
    scale = -sharpness * math.log2(math.e)

    copies = [
        pltpu.make_async_copy(centers_hbm, held.at[0, :, pl.ds(0, features)], local_sem.at[0]),
        pltpu.make_async_copy(coef_hbm, held.at[0, :, pl.ds(features, 2 * columns)], local_sem.at[1]),
        pltpu.make_async_copy(points_hbm, points, local_sem.at[2]),
    ]
    for copy in copies:
        copy.start()

    barrier = pltpu.get_barrier_semaphore()
    greet = [{"blk": left}, {"blk": right}, {"sum": other}]
    partner = {"grp": group + 1 - 2 * side}
    if cross:
        greet.append(partner)
    for device in greet:
        pl.semaphore_signal(barrier, inc=1, device_id=device, device_id_type=MESH)
    pl.semaphore_wait(barrier, len(greet))

    pieces = []
    start = 0
    only = sum(PIECES[0]) * block // 128
    base = side * (block - only) if cross else 0
    for size in (size * block // 128 for size in PIECES[0]):
        pieces.append((pl.ds(pl.multiple_of(base + start, 16), size), True))
        start += size
    start, end = only, block - only if cross else block
    sizes = [size * block // 128 for size in PIECES[1]]
    sizes[-1] = end - start - sum(sizes[:-1])
    for size in sizes:
        pieces.append((pl.ds(start, size), False))
        start += size
    count = len(pieces)

    def slot(way, d):
        if d == 0:
            return 0
        return n - 1 if d == half else 2 * d - 1 + way

    ring = {}
    for d in range(1, half + 1):
        for way in (0, 1):
            for part in range(count):
                if d == half and way != (part >= FIRST):
                    continue
                ring[way, d, part] = pltpu.make_async_remote_copy(
                    src_ref=held.at[slot(way, d - 1), pieces[part][0]],
                    dst_ref=held.at[slot(way, d), pieces[part][0]],
                    send_sem=ring_send.at[way, d - 1, part],
                    recv_sem=ring_recv.at[way, d - 1, part],
                    device_id={"blk": (right, left)[way]},
                    device_id_type=MESH,
                )
    over = {}
    if cross:
        for s in range(1, n):
            for part in range(len(PIECES[0])):
                over[s, part] = pltpu.make_async_remote_copy(
                    src_ref=held.at[s, pieces[part][0]], dst_ref=held.at[s, pieces[part][0]],
                    send_sem=x_send.at[s, part], recv_sem=x_recv.at[s, part],
                    device_id=partner, device_id_type=MESH,
                )

    def row_sums(a, b):
        return lax.dot_general(a, b, (((1,), (1,)), ((), ())), preferred_element_type=jnp.float32)

    def split_square(v):
        square = jnp.square(v.astype(jnp.float32))
        high = square.astype(jnp.bfloat16)
        return high, (square - high.astype(jnp.float32)).astype(jnp.bfloat16)

    def prepare(first, count):
        size = count * block
        c = held[first:first + count, :, 0:features].reshape(size, features)
        w = held[first:first + count, :, features:features + 2 * columns].reshape(size, 2 * columns)
        high, low = split_square(c)
        ones = jnp.ones((16, features), jnp.bfloat16)
        term = scale * (row_sums(ones, high) + row_sums(ones, low))[0:1, :]
        return c, w, term

    def tile_sum(c, w, term, at, tile):
        products = row_sums(points[pl.ds(at, tile), :], c)
        a = point_term[pl.ds(at, tile), :]
        parts = []
        for lane in range(0, c.shape[0], 128):
            exponent = (a + term[:, lane:lane + 128]) - (2.0 * scale) * products[:, lane:lane + 128]
            parts.append(jnp.exp2(exponent).astype(jnp.bfloat16))
        kernel = parts[0] if len(parts) == 1 else jnp.concatenate(parts, axis=1)
        return jnp.dot(kernel, w, preferred_element_type=jnp.float32)

    def group_sum(first, count, fresh):
        c, w, term = prepare(first, count)

        @pl.loop(0, rows // TILE)
        def _(i):
            at = pl.multiple_of(i * TILE, TILE)
            got = tile_sum(c, w, term, at, TILE)
            for h in (0, 1):
                piece = got[:, h * columns:(h + 1) * columns]
                if fresh:
                    total[h, pl.ds(at, TILE), :] = piece
                else:
                    total[h, pl.ds(at, TILE), :] += piece

    copies[0].wait()
    copies[1].wait()
    for part in range(count):
        for way in (0, 1):
            if (way, 1, part) in ring:
                ring[way, 1, part].start()

    copies[2].wait()

    @pl.loop(0, rows // TILE)
    def _(i):
        at = pl.multiple_of(i * TILE, TILE)
        high, low = split_square(points[pl.ds(at, TILE), :])
        ones = jnp.ones((128, features), jnp.bfloat16)
        point_term[pl.ds(at, TILE), :] = scale * (row_sums(high, ones) + row_sums(low, ones))

    for d in range(1, half + 1):
        for part in range(count):
            for way in (0, 1):
                if (way, d, part) not in ring:
                    continue
                ring[way, d, part].wait_recv()
                if (way, d + 1, part) in ring:
                    ring[way, d + 1, part].start()
                if cross and pieces[part][1]:
                    over[slot(way, d), part].start()
        if d == 1:
            group_sum(0, 1, True)
        else:
            if cross:
                for part in range(len(PIECES[0])):
                    over[slot(0, d - 1), part].wait_recv()
                    over[slot(1, d - 1), part].wait_recv()
            group_sum(slot(0, d - 1), 2, False)

    if cross:
        for part in range(len(PIECES[0])):
            over[n - 1, part].wait_recv()
    c, w, term = prepare(n - 1, 1)
    size = rows // CHUNKS
    swaps = []
    for i in range(CHUNKS):
        got = tile_sum(c, w, term, i * size, size)
        for h in (0, 1):
            total[h, i * size:(i + 1) * size, :] += got[:, h * columns:(h + 1) * columns]
        swap = pltpu.make_async_remote_copy(
            src_ref=total.at[other, pl.ds(i * size, size)],
            dst_ref=landed.at[pl.ds(i * size, size)],
            send_sem=swap_send.at[i], recv_sem=swap_recv.at[i],
            device_id={"sum": other}, device_id_type=MESH,
        )
        swap.start()
        swaps.append(swap)
    for i in range(CHUNKS):
        swaps[i].wait_recv()
        at = pl.ds(i * size, size)
        out_ref[at, :] = total[mine, at, :] + landed[at, :]
    for copy in (*ring.values(), *over.values(), *swaps):
        copy.wait_send()


def per_device(n, cross, points, centers, coefficients, targets):
    rows, features = points.shape
    block = centers.shape[0]
    width = coefficients.shape[1]
    columns = targets.shape[1]
    half = n // 2
    predicted = pl.pallas_call(
        functools.partial(body, n, cross),
        out_shape=pltpu.VMEM((rows, columns), jnp.float32),
        in_specs=[pl.BlockSpec(memory_space=pl.ANY)] * 3,
        out_specs=pl.BlockSpec(memory_space=pltpu.VMEM),
        scratch_shapes=[
            pltpu.VMEM((rows, features), jnp.bfloat16),
            pltpu.VMEM((n, block, features + width), jnp.bfloat16),
            pltpu.VMEM((rows, 128), jnp.float32),
            pltpu.VMEM((2, rows, columns), jnp.float32),
            pltpu.VMEM((rows, columns), jnp.float32),
            pltpu.SemaphoreType.DMA((3,)),
            pltpu.SemaphoreType.DMA((2, half, len(PIECES[0]) + len(PIECES[1]))),
            pltpu.SemaphoreType.DMA((2, half, len(PIECES[0]) + len(PIECES[1]))),
            pltpu.SemaphoreType.DMA((n, len(PIECES[0]))),
            pltpu.SemaphoreType.DMA((n, len(PIECES[0]))),
            pltpu.SemaphoreType.DMA((CHUNKS,)),
            pltpu.SemaphoreType.DMA((CHUNKS,)),
        ],
        compiler_params=pltpu.CompilerParams(
            collective_id=0, has_side_effects=True, vmem_limit_bytes=58 * 2**20
        ),
        cost_estimate=pl.CostEstimate(
            flops=2 * rows * n * block * (features + width),
            bytes_accessed=2 * rows * features + 4 * rows * columns,
            transcendentals=rows * n * block,
        ),
    )(points, centers, coefficients)
    return targets - predicted


def solution(mesh):
    return jax.shard_map(
        functools.partial(per_device, mesh.shape["blk"], mesh.shape["grp"] % 2 == 0),
        mesh=mesh,
        in_specs=(
            P(("grp", "blk"), None),
            P(("blk", "sum"), None),
            P(("blk", "sum"), None),
            P(("grp", "blk"), "sum"),
        ),
        out_specs=P(("grp", "blk"), "sum"),
        check_vma=False,
    )
```

```python
import functools
import math

import jax
import jax.numpy as jnp
from jax import lax
from jax.experimental import pallas as pl
from jax.experimental.pallas import tpu as pltpu
from jax.sharding import PartitionSpec as P

MESH = pl.DeviceIdType.MESH
TILE = 2048
CHUNKS = 4
PIECES = ((16, 32), (32,))
FIRST = 2


def ring_position(index, n):
    return jnp.where(lax.rem(index, 2) == 0, index // 2, n - 1 - index // 2) if n <= 8 else index


def ring_index(position, n):
    return jnp.where(position < n // 2, 2 * position, 2 * (n - 1 - position) + 1) if n <= 8 else position


def body(n, cross, points_hbm, centers_hbm, coef_hbm, out_ref,
         points, held, point_term, total, landed,
         local_sem, ring_send, ring_recv, x_send, x_recv, swap_send, swap_recv):
    rows, features = points.shape
    block = held.shape[1]
    columns = total.shape[2]
    half = n // 2
    me = ring_position(lax.axis_index("blk"), n)
    right = ring_index(lax.rem(me + 1, n), n)
    left = ring_index(lax.rem(me + n - 1, n), n)
    mine = lax.axis_index("sum")
    other = 1 - mine
    group = lax.axis_index("grp")
    side = lax.rem(group, 2)
    sharpness = 0.15 / math.sqrt(features)
    scale = -sharpness * math.log2(math.e)

    copies = [
        pltpu.make_async_copy(centers_hbm, held.at[0, :, pl.ds(0, features)], local_sem.at[0]),
        pltpu.make_async_copy(coef_hbm, held.at[0, :, pl.ds(features, 2 * columns)], local_sem.at[1]),
        pltpu.make_async_copy(points_hbm, points, local_sem.at[2]),
    ]
    for copy in copies:
        copy.start()

    barrier = pltpu.get_barrier_semaphore()
    greet = [{"blk": left}, {"blk": right}, {"sum": other}]
    partner = {"grp": group + 1 - 2 * side}
    if cross:
        greet.append(partner)
    for device in greet:
        pl.semaphore_signal(barrier, inc=1, device_id=device, device_id_type=MESH)
    pl.semaphore_wait(barrier, len(greet))

    pieces = []
    start = 0
    only = sum(PIECES[0]) * block // 128
    base = side * (block - only) if cross else 0
    for size in (size * block // 128 for size in PIECES[0]):
        pieces.append((pl.ds(pl.multiple_of(base + start, 16), size), True))
        start += size
    start, end = only, block - only if cross else block
    sizes = [size * block // 128 for size in PIECES[1]]
    sizes[-1] = end - start - sum(sizes[:-1])
    for size in sizes:
        pieces.append((pl.ds(start, size), False))
        start += size
    count = len(pieces)

    def slot(way, d):
        if d == 0:
            return 0
        return n - 1 if d == half else 2 * d - 1 + way

    ring = {}
    for d in range(1, half + 1):
        for way in (0, 1):
            for part in range(count):
                if d == half and way != (part >= FIRST):
                    continue
                ring[way, d, part] = pltpu.make_async_remote_copy(
                    src_ref=held.at[slot(way, d - 1), pieces[part][0]],
                    dst_ref=held.at[slot(way, d), pieces[part][0]],
                    send_sem=ring_send.at[way, d - 1, part],
                    recv_sem=ring_recv.at[way, d - 1, part],
                    device_id={"blk": (right, left)[way]},
                    device_id_type=MESH,
                )
    over = {}
    if cross:
        for s in range(1, n):
            for part in range(len(PIECES[0])):
                over[s, part] = pltpu.make_async_remote_copy(
                    src_ref=held.at[s, pieces[part][0]], dst_ref=held.at[s, pieces[part][0]],
                    send_sem=x_send.at[s, part], recv_sem=x_recv.at[s, part],
                    device_id=partner, device_id_type=MESH,
                )

    def row_sums(a, b):
        return lax.dot_general(a, b, (((1,), (1,)), ((), ())), preferred_element_type=jnp.float32)

    def split_square(v):
        square = jnp.square(v.astype(jnp.float32))
        high = square.astype(jnp.bfloat16)
        return high, (square - high.astype(jnp.float32)).astype(jnp.bfloat16)

    def prepare(first, count):
        size = count * block
        c = held[first:first + count, :, 0:features].reshape(size, features)
        w = held[first:first + count, :, features:features + 2 * columns].reshape(size, 2 * columns)
        high, low = split_square(c)
        ones = jnp.ones((16, features), jnp.bfloat16)
        term = scale * (row_sums(ones, high) + row_sums(ones, low))[0:1, :]
        return c, w, term

    def tile_sum(c, w, term, at, tile):
        products = row_sums(points[pl.ds(at, tile), :], c)
        a = point_term[pl.ds(at, tile), :]
        parts = []
        for lane in range(0, c.shape[0], 128):
            exponent = (a + term[:, lane:lane + 128]) - (2.0 * scale) * products[:, lane:lane + 128]
            parts.append(jnp.exp2(exponent).astype(jnp.bfloat16))
        kernel = parts[0] if len(parts) == 1 else jnp.concatenate(parts, axis=1)
        return jnp.dot(kernel, w, preferred_element_type=jnp.float32)

    def group_sum(first, count, fresh):
        c, w, term = prepare(first, count)

        @pl.loop(0, rows // TILE)
        def _(i):
            at = pl.multiple_of(i * TILE, TILE)
            got = tile_sum(c, w, term, at, TILE)
            for h in (0, 1):
                piece = got[:, h * columns:(h + 1) * columns]
                if fresh:
                    total[h, pl.ds(at, TILE), :] = piece
                else:
                    total[h, pl.ds(at, TILE), :] += piece

    copies[0].wait()
    copies[1].wait()
    for part in range(count):
        for way in (0, 1):
            if (way, 1, part) in ring:
                ring[way, 1, part].start()

    copies[2].wait()

    @pl.loop(0, rows // TILE)
    def _(i):
        at = pl.multiple_of(i * TILE, TILE)
        high, low = split_square(points[pl.ds(at, TILE), :])
        ones = jnp.ones((128, features), jnp.bfloat16)
        point_term[pl.ds(at, TILE), :] = scale * (row_sums(high, ones) + row_sums(low, ones))

    for d in range(1, half + 1):
        for part in range(count):
            for way in (0, 1):
                if (way, d, part) not in ring:
                    continue
                ring[way, d, part].wait_recv()
                if (way, d + 1, part) in ring:
                    ring[way, d + 1, part].start()
                if cross and pieces[part][1]:
                    over[slot(way, d), part].start()
        if d == 1:
            group_sum(0, 1, True)
        else:
            if cross:
                for part in range(len(PIECES[0])):
                    over[slot(0, d - 1), part].wait_recv()
                    over[slot(1, d - 1), part].wait_recv()
            group_sum(slot(0, d - 1), 2, False)

    if cross:
        for part in range(len(PIECES[0])):
            over[n - 1, part].wait_recv()
    c, w, term = prepare(n - 1, 1)
    size = rows // CHUNKS
    swaps = []
    for i in range(CHUNKS):
        got = tile_sum(c, w, term, i * size, size)
        for h in (0, 1):
            total[h, i * size:(i + 1) * size, :] += got[:, h * columns:(h + 1) * columns]
        swap = pltpu.make_async_remote_copy(
            src_ref=total.at[other, pl.ds(i * size, size)],
            dst_ref=landed.at[pl.ds(i * size, size)],
            send_sem=swap_send.at[i], recv_sem=swap_recv.at[i],
            device_id={"sum": other}, device_id_type=MESH,
        )
        swap.start()
        swaps.append(swap)
    for i in range(CHUNKS):
        swaps[i].wait_recv()
        at = pl.ds(i * size, size)
        out_ref[at, :] = total[mine, at, :] + landed[at, :]
    for copy in (*ring.values(), *over.values(), *swaps):
        copy.wait_send()


def per_device(n, cross, points, centers, coefficients, targets):
    rows, features = points.shape
    block = centers.shape[0]
    width = coefficients.shape[1]
    columns = targets.shape[1]
    half = n // 2
    predicted = pl.pallas_call(
        functools.partial(body, n, cross),
        out_shape=pltpu.VMEM((rows, columns), jnp.float32),
        in_specs=[pl.BlockSpec(memory_space=pl.ANY)] * 3,
        out_specs=pl.BlockSpec(memory_space=pltpu.VMEM),
        scratch_shapes=[
            pltpu.VMEM((rows, features), jnp.bfloat16),
            pltpu.VMEM((n, block, features + width), jnp.bfloat16),
            pltpu.VMEM((rows, 128), jnp.float32),
            pltpu.VMEM((2, rows, columns), jnp.float32),
            pltpu.VMEM((rows, columns), jnp.float32),
            pltpu.SemaphoreType.DMA((3,)),
            pltpu.SemaphoreType.DMA((2, half, len(PIECES[0]) + len(PIECES[1]))),
            pltpu.SemaphoreType.DMA((2, half, len(PIECES[0]) + len(PIECES[1]))),
            pltpu.SemaphoreType.DMA((n, len(PIECES[0]))),
            pltpu.SemaphoreType.DMA((n, len(PIECES[0]))),
            pltpu.SemaphoreType.DMA((CHUNKS,)),
            pltpu.SemaphoreType.DMA((CHUNKS,)),
        ],
        compiler_params=pltpu.CompilerParams(
            collective_id=0, has_side_effects=True, vmem_limit_bytes=58 * 2**20
        ),
        cost_estimate=pl.CostEstimate(
            flops=2 * rows * n * block * (features + width),
            bytes_accessed=2 * rows * features + 4 * rows * columns,
            transcendentals=rows * n * block,
        ),
    )(points, centers, coefficients)
    return targets - predicted


def solution(mesh):
    return jax.shard_map(
        functools.partial(per_device, mesh.shape["blk"], mesh.shape["grp"] % 2 == 0),
        mesh=mesh,
        in_specs=(
            P(("grp", "blk"), None),
            P(("blk", "sum"), None),
            P(("blk", "sum"), None),
            P(("grp", "blk"), "sum"),
        ),
        out_specs=P(("grp", "blk"), "sum"),
        check_vma=False,
    )
```
